32 devices in a mesh: gx: 8 (over z, y), gz: 4 (over x, core).
Axes of the slice: x: 2, y: 2, z: 4, core: 2. Of those that a mesh axis runs over, the one named last changes fastest.
Arguments:
- field: float32 [4, 4, 512, 1024], P(None, 'gz', None, 'gx'), may hold values from -6 to 6
- drop_cell: int32 [131072], P(('gx', 'gz')), may hold values from 0 to 65535
- drop_plane: int32 [131072], P(('gx', 'gz')), may hold values from 0 to 3
- drop_rate: float32 [2, 131072], P(None, ('gx', 'gz')), may hold values from -8 to 8
- diffusivity: float32 [4], replicated, may hold values from 0.25 to 4
- wall_eigen: float32 [512], replicated, may hold values from 0.05 to 2
- basis_part: float32 [512, 512], replicated, may hold values from -0.125 to 0.125
- dual_part: float32 [512, 512], replicated, may hold values from -0.125 to 0.125
- bulk_shift: float32 [1], replicated, may hold values from 2.2 to 2.8
Outputs:
- new_field: float32 [4, 4, 512, 1024], P(None, 'gz', None, 'gx')
The draws below stay inside these ranges and needn't reach their ends.
All inputs are finite; a program needn't handle non-finite values.
Results may differ from the reference program's by a relative error of at most 0.0001.
Values sent between devices are 32-bit elements; how exact they have to be, the bound alone decides.
A program may use at most 64 MiB of HBM per device.

```python
import math
import jax
import jax.numpy as jnp
from jax import lax

F = 4
Y = 512
XD = 128
NX = 1024
PLANES = 4
SLAB_DROPS = 16384
DROPS = 131072


def with_ends(entries, rng, least, top_value):
    index_at = [jax.random.randint(jax.random.fold_in(rng, axis), (), 0, length) for axis, length in enumerate(entries.shape)]
    main_axis = entries.shape.index(max(entries.shape))
    neighbour = index_at[:main_axis] + [(index_at[main_axis] + 1) % entries.shape[main_axis]] + index_at[main_axis + 1:]
    return entries.at[tuple(index_at)].set(least).at[tuple(neighbour)].set(top_value)


def block_levels(key, dims, shards, smallest, top_value):
    loudness = 1.0
    for axis_at, shards_of in shards:
        heights = jax.random.uniform(jax.random.fold_in(jax.random.fold_in(key, 6), axis_at), (shards_of,), jnp.float32, smallest / len(shards), top_value / len(shards))
        loudness = loudness * jnp.repeat(jnp.exp(heights), dims[axis_at] // shards_of).reshape((-1,) + (1,) * (len(dims) - 1 - axis_at))
    return loudness


def gaussian(stream_key, shape, width, bound, pieces=(), kind=jnp.bfloat16):
    result = width * jax.random.normal(stream_key, shape, jnp.float32)
    if pieces:
        result = result * block_levels(stream_key, shape, pieces, -0.22, 0.18)
    return jnp.clip(result, -bound, bound).astype(kind)


def setup_inputs(seed: int = 0) -> dict:
    key_of = jax.random.split(jax.random.key(seed), 10)
    return {
        "field": gaussian(key_of[0], (F, PLANES, Y, NX), 1.0, 6.0, ((1, 4), (3, 8)), jnp.float32),
        "drop_cell": with_ends(jax.random.randint(key_of[1], (DROPS,), 0, Y * XD), jax.random.fold_in(key_of[1], 1), 0, (Y * XD) - 1).astype(jnp.int32),
        "drop_plane": with_ends(jax.random.randint(key_of[2], (DROPS,), 0, PLANES), jax.random.fold_in(key_of[2], 1), 0, PLANES - 1).astype(jnp.int32),
        "drop_rate": gaussian(key_of[3], (2, DROPS), 2.0, 8.0, ((1, 32),), jnp.float32),
        "diffusivity": jnp.clip(jnp.exp(jax.random.uniform(key_of[4], (F,), jnp.float32, math.log(0.25), math.log(4.0))), 0.25, 4.0),
        "wall_eigen": jnp.clip(jnp.exp(jax.random.uniform(key_of[5], (Y,), jnp.float32, math.log(0.05), math.log(2.0))), 0.05, 2.0),
        "basis_part": gaussian(key_of[6], (Y, Y), (4 * Y) ** -0.5, 0.125, (), jnp.float32),
        "dual_part": gaussian(key_of[7], (Y, Y), (4 * Y) ** -0.5, 0.125, (), jnp.float32),
        "bulk_shift": jnp.clip(jax.random.uniform(key_of[8], (1,), jnp.float32, 2.2, 2.8), 2.2, 2.8),
    }


def reference(field, drop_cell, drop_plane, drop_rate, diffusivity, wall_eigen, basis_part, dual_part, bulk_shift):
    droplet_index = jnp.arange(DROPS, dtype=jnp.int32)
    slab_index = droplet_index // SLAB_DROPS
    column_index = slab_index * XD + drop_cell % XD
    height_index = drop_cell // XD
    flat_cell = ((drop_plane * Y + height_index) * NX + column_index).astype(jnp.int32)
    source = jnp.stack([jax.ops.segment_sum(drop_rate[component], flat_cell, num_segments=PLANES * Y * NX) for component in range(2)])
    source = source.reshape(2, PLANES, Y, NX)
    right_side = jnp.concatenate([field[:2], field[2:] + source], axis=0)
    identity = jnp.eye(Y, dtype=jnp.float32)
    dual_full = identity + dual_part
    basis_full = identity + basis_part
    mode_index = jnp.arange(NX, dtype=jnp.int32)
    folded = jnp.minimum(mode_index, NX - mode_index).astype(jnp.float32)
    wavenumber = (2.0 * math.pi / NX) * folded
    signed = jnp.where(2 * mode_index >= NX, mode_index - NX, mode_index).astype(jnp.float32)
    travel = (2.0 * math.pi / NX) * signed * bulk_shift[0]
    results = []
    for field_number in range(F):
        projected = jnp.einsum('ay,zyx->zax', dual_full, right_side[field_number], precision=lax.Precision.HIGHEST)
        spectrum = jnp.fft.fft(projected, axis=-1)
        growth = diffusivity[field_number] * (wall_eigen[:, None] + wavenumber[None, :] ** 2)
        damping = (1.0 - growth) / (1.0 + growth)
        factor = lax.complex(damping * jnp.cos(travel)[None, :], -damping * jnp.sin(travel)[None, :])
        filtered = jnp.real(jnp.fft.ifft(spectrum * factor[None], axis=-1))
        results.append(jnp.einsum('ya,zax->zyx', basis_full, filtered, precision=lax.Precision.HIGHEST))
    return jnp.stack(results)
```

```python
import functools
import math

import jax
import jax.numpy as jnp
import numpy as np
from jax import lax
from jax.experimental import pallas as pl
from jax.experimental.pallas import tpu as pltpu
from jax.sharding import PartitionSpec as P

DENSE_LIMIT = 2048


def real_table(total):
    half = total // 2
    product = np.arange(total)[:, None] * np.arange(half)[None, :] % total
    angle = 2.0 * np.pi / total * product
    sines = -np.sin(angle)
    sines[:, 0] = 1.0 - 2.0 * (np.arange(total) % 2)
    return np.concatenate([np.cos(angle), sines], axis=1).astype(np.float32)


def deposit_kernel(slab_width, row_ref, col_ref, rate_ref, out_ref):
    rows = out_ref.shape[0]
    depth = row_ref.shape[1]

    @pl.when(pl.program_id(0) == 0)
    def _():
        out_ref[...] = jnp.zeros_like(out_ref)

    hit = lax.broadcasted_iota(jnp.int32, (rows, depth), 0) == row_ref[...]
    left = jnp.where(hit, 1.0, 0.0).astype(jnp.bfloat16)
    here = lax.broadcasted_iota(jnp.int32, (slab_width, depth), 0) == col_ref[...]
    terms = []
    for component in range(2):
        rate = rate_ref[component : component + 1, :]
        high = rate.astype(jnp.bfloat16).astype(jnp.float32)
        for part in (high, rate - high):
            terms.append(jnp.where(here, part, 0.0).astype(jnp.bfloat16))
    right = jnp.concatenate(terms, axis=0)
    out_ref[...] += lax.dot_general(
        left, right, (((1,), (1,)), ((), ())), preferred_element_type=jnp.float32
    )


def deposit(row, col, rate, row_count, slab_width):
    drops = row.shape[1]
    block = min(2048, drops)
    out = pl.pallas_call(
        functools.partial(deposit_kernel, slab_width),
        grid=(drops // block,),
        in_specs=[
            pl.BlockSpec((1, block), lambda i: (0, i)),
            pl.BlockSpec((1, block), lambda i: (0, i)),
            pl.BlockSpec((2, block), lambda i: (0, i)),
        ],
        out_specs=pl.BlockSpec((row_count, 4 * slab_width), lambda i: (0, 0)),
        out_shape=jax.ShapeDtypeStruct((row_count, 4 * slab_width), jnp.float32),
        compiler_params=pltpu.CompilerParams(vmem_limit_bytes=40 * 2**20),
    )(row, col, rate)
    parts = out.reshape(row_count, 2, 2, slab_width).sum(axis=2)
    return parts.transpose(1, 0, 2)


def damping_of(diffusivity, eigen_rows, mode_index, total_cells):
    wavenumber = 2.0 * math.pi / total_cells * mode_index.astype(jnp.float32)
    growth = diffusivity[:, None, None] * (
        eigen_rows[None, :, None] + wavenumber[None, None, :] ** 2
    )
    return (1.0 - growth) / (1.0 + growth)


def per_device(
    field, drop_cell, drop_plane, drop_rate, diffusivity, wall_eigen, basis_part, dual_part, bulk_shift
):
    field_count, _, row_count, slab_width = field.shape
    gx_count = lax.axis_size("gx")
    total = slab_width * gx_count
    own_rows = row_count // gx_count
    half = total // 2
    field = field[:, 0]
    drops = jnp.concatenate(
        [
            drop_cell.astype(jnp.float32)[None],
            drop_plane.astype(jnp.float32)[None],
            drop_rate,
        ]
    )
    drops = lax.all_gather(drops, "gz", axis=1, tiled=True)
    cell = drops[0].astype(jnp.int32)
    mine = drops[1].astype(jnp.int32) == lax.axis_index("gz")
    row = jnp.where(mine, cell // slab_width, -1)[None]
    col = (cell % slab_width)[None]
    source = deposit(row, col, drops[2:], row_count, slab_width)

    def project(matrix, values):
        return values + jnp.einsum("ay,fyx->fax", matrix, values, precision=lax.Precision.HIGH)

    def scatter_rows(values):
        pieces = values.reshape(values.shape[0], gx_count, own_rows, slab_width)
        return lax.all_to_all(pieces, "gx", 1, 1, tiled=True)

    position = lax.axis_index("gx")
    eigen = lax.dynamic_slice(wall_eigen, (position * own_rows,), (own_rows,))
    mode = jnp.arange(half, dtype=jnp.int32)
    damping = damping_of(diffusivity, eigen, mode, total)
    last = damping_of(diffusivity, eigen, jnp.full((1,), half, jnp.int32), total)
    travel = 2.0 * math.pi / total * mode.astype(jnp.float32) * bulk_shift[0]
    last_cos = jnp.cos(-math.pi * bulk_shift[0])

    def filter_rows(values, first):
        count = values.shape[0]
        damp = damping[first : first + count]
        end = last[first : first + count]
        if total <= DENSE_LIMIT:
            table = jnp.asarray(real_table(total)).reshape(gx_count, slab_width, total)
            spec = jnp.einsum("fsaj,sjk->fak", values, table, precision=lax.Precision.HIGH)
            real, imag = spec[..., :half], spec[..., half:]
            weight = jnp.where(mode == 0, 1.0, 2.0) / total
            cosine = damp * (weight * jnp.cos(travel))
            sine = damp * (weight * jnp.sin(travel))
            turned = jnp.where(mode == 0, end * (last_cos / total), cosine)
            spec = jnp.concatenate(
                [real * cosine + imag * sine, imag * turned - real * sine], axis=-1
            )
            return jnp.einsum("fak,sjk->fsaj", spec, table, precision=lax.Precision.HIGH)
        flat = values.transpose(0, 2, 1, 3).reshape(count, own_rows, total)
        spec = jnp.fft.rfft(flat, axis=-1)
        full = jnp.concatenate([damp, end], axis=-1)
        angle = jnp.append(travel, -math.pi * bulk_shift[0])
        spec = spec * lax.complex(full * jnp.cos(angle), -full * jnp.sin(angle))
        back = jnp.fft.irfft(spec, n=total, axis=-1)
        return back.reshape(count, own_rows, gx_count, slab_width).transpose(0, 2, 1, 3)

    parts = []
    for first, group in ((0, field[:2]), (2, field[2:] + source)):
        rows = scatter_rows(project(dual_part, group))
        back = scatter_rows(filter_rows(rows, first))
        filtered = back.reshape(group.shape)
        parts.append(project(basis_part, filtered))
    return jnp.concatenate(parts)[:, None]


def solution(mesh):
    in_specs = (
        P(None, "gz", None, "gx"),
        P(("gx", "gz")),
        P(("gx", "gz")),
        P(None, ("gx", "gz")),
        P(),
        P(),
        P(),
        P(),
        P(),
    )
    out_specs = P(None, "gz", None, "gx")
    return jax.shard_map(
        per_device, mesh=mesh, in_specs=in_specs, out_specs=out_specs, check_vma=False
    )
```

```python
import functools
import math

import jax
import jax.numpy as jnp
import numpy as np
from jax import lax
from jax.experimental import pallas as pl
from jax.experimental.pallas import tpu as pltpu
from jax.sharding import PartitionSpec as P

DENSE_PARTS = 16


def real_table(total):
    half = total // 2
    product = np.arange(total)[:, None] * np.arange(half)[None, :] % total
    angle = 2.0 * np.pi / total * product
    sines = -np.sin(angle)
    sines[:, 0] = 1.0 - 2.0 * (np.arange(total) % 2)
    return np.concatenate([np.cos(angle), sines], axis=1).astype(np.float32)


def split_two(values):
    high = values.astype(jnp.bfloat16)
    return high, (values - high.astype(jnp.float32)).astype(jnp.bfloat16)


def product(left, right, transposed=False):
    return lax.dot_general(
        left,
        right,
        (((1,), (1 if transposed else 0,)), ((), ())),
        preferred_element_type=jnp.float32,
    )


def step_kernel(
    gx_count,
    gz_count,
    field_ref,
    drop_ref,
    dual_ref,
    basis_ref,
    eigen_ref,
    aux_ref,
    high_hbm,
    low_hbm,
    out_ref,
    high_ref,
    low_ref,
    matrix_ref,
    gathered,
    total_ref,
    send_one,
    recv_one,
    send_two,
    recv_two,
    drop_send,
    drop_recv,
    one_send,
    one_recv,
    two_send,
    two_recv,
    load_sem,
):
    field_count, row_count, slab_width = field_ref.shape
    own_rows = row_count // gx_count
    pairs = field_count // 2
    half = gx_count * slab_width // 2
    me = lax.axis_index("gx")
    plane = lax.axis_index("gz")

    barrier = pltpu.get_barrier_semaphore()
    for off in range(1, gx_count):
        pl.semaphore_signal(
            barrier,
            inc=1,
            device_id=(lax.rem(me + off, gx_count), plane),
            device_id_type=pl.DeviceIdType.MESH,
        )
    for off in range(1, gz_count):
        pl.semaphore_signal(
            barrier,
            inc=1,
            device_id=(me, lax.rem(plane + off, gz_count)),
            device_id_type=pl.DeviceIdType.MESH,
        )
    pl.semaphore_wait(barrier, gx_count + gz_count - 2)

    drop_copies = []
    for off in range(1, gz_count):
        copy = pltpu.make_async_remote_copy(
            src_ref=drop_ref,
            dst_ref=gathered.at[off],
            send_sem=drop_send.at[off],
            recv_sem=drop_recv.at[off],
            device_id=(me, lax.rem(plane + off, gz_count)),
            device_id_type=pl.DeviceIdType.MESH,
        )
        copy.start()
        drop_copies.append(copy)
    loads = [
        pltpu.make_async_copy(high_hbm, high_ref, load_sem.at[0]),
        pltpu.make_async_copy(low_hbm, low_ref, load_sem.at[1]),
    ]
    for copy in loads:
        copy.start()

    def load_matrix(ref):
        high, low = split_two(ref[...])
        matrix_ref[:, :row_count] = high
        matrix_ref[:, row_count : 2 * row_count] = low
        matrix_ref[:, 2 * row_count :] = high

    def apply_matrix(values):
        high, low = split_two(values)
        return values + product(matrix_ref[...], jnp.concatenate([high, high, low], axis=0))

    def exchange(pair, source, landing, send_sem, recv_sem):
        copies = []
        for off in range(1, gx_count):
            target = lax.rem(me + off, gx_count)
            copy = pltpu.make_async_remote_copy(
                src_ref=source.at[pl.ds(2 * pair, 2), target],
                dst_ref=landing.at[pl.ds(2 * pair, 2), me],
                send_sem=send_sem.at[pair * gx_count + off],
                recv_sem=recv_sem.at[pair * gx_count + off],
                device_id=(target, plane),
                device_id_type=pl.DeviceIdType.MESH,
            )
            copy.start()
            copies.append(copy)
        landing[pl.ds(2 * pair, 2), me] = source[pl.ds(2 * pair, 2), me]
        return copies

    def project(pair, values):
        values = apply_matrix(values)
        for side in range(2):
            send_one[2 * pair + side] = values[
                :, side * slab_width : (side + 1) * slab_width
            ].reshape(gx_count, own_rows, slab_width)
        return exchange(pair, send_one, recv_one, one_send, one_recv)

    load_matrix(dual_ref)
    first = [project(0, jnp.concatenate([field_ref[0], field_ref[1]], axis=1))]

    gathered[0] = drop_ref[...]
    total_ref[...] = jnp.zeros_like(total_ref)
    for copy in drop_copies:
        copy.wait()
    drops = drop_ref.shape[1]
    block = min(2048, drops)
    blocks = drops // block

    def deposit(step, carry):
        packet = gathered[step // blocks, :, pl.ds(pl.multiple_of(step % blocks * block, 128), block)]
        cell = packet[0:1].astype(jnp.int32)
        mine = packet[1:2].astype(jnp.int32) == plane
        row = jnp.where(mine, cell // slab_width, -1)
        col = cell % slab_width
        hit = lax.broadcasted_iota(jnp.int32, (row_count, block), 0) == row
        left = jnp.where(hit, 1.0, 0.0).astype(jnp.bfloat16)
        here = lax.broadcasted_iota(jnp.int32, (slab_width, block), 0) == col
        terms = []
        for component in range(2):
            rate = packet[2 + component : 3 + component]
            high = rate.astype(jnp.bfloat16).astype(jnp.float32)
            for part in (high, rate - high):
                terms.append(jnp.where(here, part, 0.0).astype(jnp.bfloat16))
        total_ref[...] += product(left, jnp.concatenate(terms, axis=0), transposed=True)
        return carry

    lax.fori_loop(0, gz_count * blocks, deposit, 0)
    merged = []
    for component in range(2):
        base = 2 * component * slab_width
        merged.append(
            field_ref[2 + component]
            + total_ref[:, base : base + slab_width]
            + total_ref[:, base + slab_width : base + 2 * slab_width]
        )
    first.append(project(1, jnp.concatenate(merged, axis=1)))
    load_matrix(basis_ref)

    for copy in loads:
        copy.wait()
    eigen = eigen_ref[pl.ds(pl.multiple_of(me * own_rows, 8), own_rows), :]
    second = []
    for pair in range(pairs):
        damps = []
        for which in range(2):
            growth = jnp.concatenate(
                [
                    aux_ref[5 + 2 * pair + side : 6 + 2 * pair + side, :]
                    * (eigen + aux_ref[which : which + 1, :])
                    for side in range(2)
                ],
                axis=0,
            )
            damps.append((1.0 - growth) / (1.0 + growth))
        cosine = damps[0] * aux_ref[2:3, :]
        sine = damps[0] * aux_ref[3:4, :]
        turned = damps[1] * aux_ref[4:5, :]
        for copy in first[pair]:
            copy.wait()
        rows = jnp.concatenate(
            [
                recv_one[2 * pair : 2 * pair + 2, slab].reshape(2 * own_rows, slab_width)
                for slab in range(gx_count)
            ],
            axis=1,
        )
        high, low = split_two(rows)
        spec = product(high, high_ref[...]) + product(low, high_ref[...])
        spec += product(high, low_ref[...])
        real, imag = spec[:, :half], spec[:, half:]
        spec = jnp.concatenate([real * cosine + imag * sine, imag * turned - real * sine], axis=1)
        high, low = split_two(spec)
        back = product(high, high_ref[...], True) + product(low, high_ref[...], True)
        back += product(high, low_ref[...], True)
        for slab in range(gx_count):
            send_two[2 * pair : 2 * pair + 2, slab] = back[
                :, slab * slab_width : (slab + 1) * slab_width
            ].reshape(2, own_rows, slab_width)
        second.append(exchange(pair, send_two, recv_two, two_send, two_recv))
    for pair in range(pairs):
        for copy in second[pair]:
            copy.wait()
        values = apply_matrix(
            jnp.concatenate(
                [recv_two[2 * pair + side].reshape(row_count, slab_width) for side in range(2)],
                axis=1,
            )
        )
        for side in range(2):
            out_ref[2 * pair + side] = values[:, side * slab_width : (side + 1) * slab_width]


def dense_step(
    field, drop_cell, drop_plane, drop_rate, diffusivity, wall_eigen, basis_part, dual_part, bulk_shift
):
    field_count, _, row_count, slab_width = field.shape
    gx_count = lax.axis_size("gx")
    gz_count = lax.axis_size("gz")
    total = slab_width * gx_count
    half = total // 2
    own_rows = row_count // gx_count
    drops = jnp.concatenate(
        [
            drop_cell.astype(jnp.float32)[None],
            drop_plane.astype(jnp.float32)[None],
            drop_rate,
        ]
    )
    mode = np.arange(half)
    wave = (2.0 * np.pi / total * mode).astype(np.float32)
    square = wave * wave
    ends = np.where(mode == 0, np.float32(np.pi) ** 2, square).astype(np.float32)
    weight = (np.where(mode == 0, 1.0, 2.0) / total).astype(np.float32)
    travel = jnp.asarray(wave) * bulk_shift[0]
    cosine = jnp.asarray(weight) * jnp.cos(travel)
    sine = jnp.asarray(weight) * jnp.sin(travel)
    turned = jnp.where(jnp.asarray(mode == 0), jnp.cos(-math.pi * bulk_shift[0]) / total, cosine)
    aux = jnp.concatenate(
        [
            jnp.stack([jnp.asarray(square), jnp.asarray(ends), cosine, sine, turned]),
            jnp.broadcast_to(diffusivity[:, None], (field_count, half)),
        ]
    )
    table = real_table(total)
    high = table.astype(jnp.bfloat16)
    low = (table - high.astype(np.float32)).astype(jnp.bfloat16)
    piece = (field_count, gx_count, own_rows, slab_width)
    vmem = pl.BlockSpec(memory_space=pltpu.VMEM)
    hbm = pl.BlockSpec(memory_space=pl.ANY)
    links = field_count // 2 * gx_count
    out = pl.pallas_call(
        functools.partial(step_kernel, gx_count, gz_count),
        out_shape=jax.ShapeDtypeStruct((field_count, row_count, slab_width), jnp.float32),
        in_specs=[vmem] * 6 + [hbm] * 2,
        out_specs=vmem,
        scratch_shapes=[
            pltpu.VMEM((total, total), jnp.bfloat16),
            pltpu.VMEM((total, total), jnp.bfloat16),
            pltpu.VMEM((row_count, 3 * row_count), jnp.bfloat16),
            pltpu.VMEM((gz_count,) + drops.shape, jnp.float32),
            pltpu.VMEM((row_count, 4 * slab_width), jnp.float32),
            pltpu.VMEM(piece, jnp.float32),
            pltpu.VMEM(piece, jnp.float32),
            pltpu.VMEM(piece, jnp.float32),
            pltpu.VMEM(piece, jnp.float32),
            pltpu.SemaphoreType.DMA((gz_count,)),
            pltpu.SemaphoreType.DMA((gz_count,)),
            pltpu.SemaphoreType.DMA((links,)),
            pltpu.SemaphoreType.DMA((links,)),
            pltpu.SemaphoreType.DMA((links,)),
            pltpu.SemaphoreType.DMA((links,)),
            pltpu.SemaphoreType.DMA((2,)),
        ],
        compiler_params=pltpu.CompilerParams(
            collective_id=0, has_side_effects=True, vmem_limit_bytes=48 * 2**20
        ),
    )(
        field.reshape(field_count, row_count, slab_width),
        drops,
        dual_part,
        basis_part,
        wall_eigen[:, None],
        aux,
        jnp.asarray(high),
        jnp.asarray(low),
    )
    return out[:, None]


def deposit_kernel(slab_width, row_ref, col_ref, rate_ref, out_ref):
    rows = out_ref.shape[0]
    depth = row_ref.shape[1]

    @pl.when(pl.program_id(0) == 0)
    def _():
        out_ref[...] = jnp.zeros_like(out_ref)

    hit = lax.broadcasted_iota(jnp.int32, (rows, depth), 0) == row_ref[...]
    left = jnp.where(hit, 1.0, 0.0).astype(jnp.bfloat16)
    here = lax.broadcasted_iota(jnp.int32, (slab_width, depth), 0) == col_ref[...]
    terms = []
    for component in range(2):
        rate = rate_ref[component : component + 1, :]
        high = rate.astype(jnp.bfloat16).astype(jnp.float32)
        for part in (high, rate - high):
            terms.append(jnp.where(here, part, 0.0).astype(jnp.bfloat16))
    right = jnp.concatenate(terms, axis=0)
    out_ref[...] += lax.dot_general(
        left, right, (((1,), (1,)), ((), ())), preferred_element_type=jnp.float32
    )


def deposit(row, col, rate, row_count, slab_width):
    drops = row.shape[1]
    block = min(2048, drops)
    out = pl.pallas_call(
        functools.partial(deposit_kernel, slab_width),
        grid=(drops // block,),
        in_specs=[
            pl.BlockSpec((1, block), lambda i: (0, i)),
            pl.BlockSpec((1, block), lambda i: (0, i)),
            pl.BlockSpec((2, block), lambda i: (0, i)),
        ],
        out_specs=pl.BlockSpec((row_count, 4 * slab_width), lambda i: (0, 0)),
        out_shape=jax.ShapeDtypeStruct((row_count, 4 * slab_width), jnp.float32),
        compiler_params=pltpu.CompilerParams(vmem_limit_bytes=40 * 2**20),
    )(row, col, rate)
    parts = out.reshape(row_count, 2, 2, slab_width).sum(axis=2)
    return parts.transpose(1, 0, 2)


def damping_of(diffusivity, eigen_rows, mode_index, total_cells):
    wavenumber = 2.0 * math.pi / total_cells * mode_index.astype(jnp.float32)
    growth = diffusivity[:, None, None] * (
        eigen_rows[None, :, None] + wavenumber[None, None, :] ** 2
    )
    return (1.0 - growth) / (1.0 + growth)


def per_device(
    field, drop_cell, drop_plane, drop_rate, diffusivity, wall_eigen, basis_part, dual_part, bulk_shift
):
    field_count, _, row_count, slab_width = field.shape
    gx_count = lax.axis_size("gx")
    total = slab_width * gx_count
    own_rows = row_count // gx_count
    half = total // 2
    field = field[:, 0]
    drops = jnp.concatenate(
        [
            drop_cell.astype(jnp.float32)[None],
            drop_plane.astype(jnp.float32)[None],
            drop_rate,
        ]
    )
    drops = lax.all_gather(drops, "gz", axis=1, tiled=True)
    cell = drops[0].astype(jnp.int32)
    mine = drops[1].astype(jnp.int32) == lax.axis_index("gz")
    row = jnp.where(mine, cell // slab_width, -1)[None]
    col = (cell % slab_width)[None]
    source = deposit(row, col, drops[2:], row_count, slab_width)

    def project(matrix, values):
        return values + jnp.einsum("ay,fyx->fax", matrix, values, precision=lax.Precision.HIGH)

    def scatter_rows(values):
        pieces = values.reshape(values.shape[0], gx_count, own_rows, slab_width)
        return lax.all_to_all(pieces, "gx", 1, 1, tiled=True)

    position = lax.axis_index("gx")
    eigen = lax.dynamic_slice(wall_eigen, (position * own_rows,), (own_rows,))
    mode = jnp.arange(half, dtype=jnp.int32)
    damping = damping_of(diffusivity, eigen, mode, total)
    last = damping_of(diffusivity, eigen, jnp.full((1,), half, jnp.int32), total)
    travel = 2.0 * math.pi / total * mode.astype(jnp.float32) * bulk_shift[0]

    def filter_rows(values, first):
        count = values.shape[0]
        damp = damping[first : first + count]
        end = last[first : first + count]
        flat = values.transpose(0, 2, 1, 3).reshape(count, own_rows, total)
        spec = jnp.fft.rfft(flat, axis=-1)
        full = jnp.concatenate([damp, end], axis=-1)
        angle = jnp.append(travel, -math.pi * bulk_shift[0])
        spec = spec * lax.complex(full * jnp.cos(angle), -full * jnp.sin(angle))
        back = jnp.fft.irfft(spec, n=total, axis=-1)
        return back.reshape(count, own_rows, gx_count, slab_width).transpose(0, 2, 1, 3)

    parts = []
    for first, group in ((0, field[:2]), (2, field[2:] + source)):
        rows = scatter_rows(project(dual_part, group))
        back = scatter_rows(filter_rows(rows, first))
        filtered = back.reshape(group.shape)
        parts.append(project(basis_part, filtered))
    return jnp.concatenate(parts)[:, None]


def solution(mesh):
    in_specs = (
        P(None, "gz", None, "gx"),
        P(("gx", "gz")),
        P(("gx", "gz")),
        P(None, ("gx", "gz")),
        P(),
        P(),
        P(),
        P(),
        P(),
    )
    out_specs = P(None, "gz", None, "gx")
    body = dense_step if mesh.shape["gx"] <= DENSE_PARTS else per_device
    return jax.shard_map(
        body, mesh=mesh, in_specs=in_specs, out_specs=out_specs, check_vma=False
    )
```

```python
import functools
import math

import jax
import jax.numpy as jnp
import numpy as np
from jax import lax
from jax.experimental import pallas as pl
from jax.experimental.pallas import tpu as pltpu
from jax.sharding import PartitionSpec as P

DENSE_PARTS = 16


def real_table(total):
    half = total // 2
    product = np.arange(total)[:, None] * np.arange(half)[None, :] % total
    angle = 2.0 * np.pi / total * product
    sines = -np.sin(angle)
    sines[:, 0] = 1.0 - 2.0 * (np.arange(total) % 2)
    return np.concatenate([np.cos(angle), sines], axis=1).astype(np.float32)


def split_two(values):
    high = values.astype(jnp.bfloat16)
    return high, (values - high.astype(jnp.float32)).astype(jnp.bfloat16)


def product(left, right, transposed=False):
    return lax.dot_general(
        left,
        right,
        (((1,), (1 if transposed else 0,)), ((), ())),
        preferred_element_type=jnp.float32,
    )


def step_kernel(
    gx_count,
    gz_count,
    cell_ref,
    plane_ref,
    rate_ref,
    eigen_ref,
    aux_ref,
    diffusivity_ref,
    shift_ref,
    field_hbm,
    dual_hbm,
    basis_hbm,
    high_hbm,
    low_hbm,
    out_ref,
    field_ref,
    dual_ref,
    basis_ref,
    drop_ref,
    high_ref,
    low_ref,
    matrix_ref,
    gathered,
    total_ref,
    send_one,
    recv_one,
    send_two,
    recv_two,
    drop_send,
    drop_recv,
    one_send,
    one_recv,
    two_send,
    two_recv,
    load_sem,
):
    field_count, row_count, slab_width = field_ref.shape
    own_rows = row_count // gx_count
    pairs = field_count // 2
    half = gx_count * slab_width // 2
    me = lax.axis_index("gx")
    plane = lax.axis_index("gz")

    loads = [
        pltpu.make_async_copy(dual_hbm, dual_ref, load_sem.at[0]),
        pltpu.make_async_copy(field_hbm, field_ref, load_sem.at[1]),
        pltpu.make_async_copy(basis_hbm, basis_ref, load_sem.at[2]),
        pltpu.make_async_copy(high_hbm, high_ref, load_sem.at[3]),
        pltpu.make_async_copy(low_hbm, low_ref, load_sem.at[4]),
    ]
    for copy in loads:
        copy.start()
    barrier = pltpu.get_barrier_semaphore()
    for off in range(1, gx_count):
        pl.semaphore_signal(
            barrier,
            inc=1,
            device_id=(lax.rem(me + off, gx_count), plane),
            device_id_type=pl.DeviceIdType.MESH,
        )
    for off in range(1, gz_count):
        pl.semaphore_signal(
            barrier,
            inc=1,
            device_id=(me, lax.rem(plane + off, gz_count)),
            device_id_type=pl.DeviceIdType.MESH,
        )
    drop_ref[0:1] = cell_ref[...].astype(jnp.float32)
    drop_ref[1:2] = plane_ref[...].astype(jnp.float32)
    drop_ref[2:4] = rate_ref[...]
    pl.semaphore_wait(barrier, gx_count + gz_count - 2)

    drop_copies = []
    for off in range(1, gz_count):
        copy = pltpu.make_async_remote_copy(
            src_ref=drop_ref,
            dst_ref=gathered.at[off],
            send_sem=drop_send.at[off],
            recv_sem=drop_recv.at[off],
            device_id=(me, lax.rem(plane + off, gz_count)),
            device_id_type=pl.DeviceIdType.MESH,
        )
        copy.start()
        drop_copies.append(copy)

    def load_matrix(ref):
        high, low = split_two(ref[...])
        matrix_ref[:, :row_count] = high
        matrix_ref[:, row_count : 2 * row_count] = low
        matrix_ref[:, 2 * row_count :] = high

    def apply_matrix(values):
        high, low = split_two(values)
        return values + product(matrix_ref[...], jnp.concatenate([high, high, low], axis=0))

    def exchange(pair, source, landing, send_sem, recv_sem):
        copies = []
        for off in range(1, gx_count):
            target = lax.rem(me + off, gx_count)
            copy = pltpu.make_async_remote_copy(
                src_ref=source.at[pl.ds(2 * pair, 2), target],
                dst_ref=landing.at[pl.ds(2 * pair, 2), me],
                send_sem=send_sem.at[pair * gx_count + off],
                recv_sem=recv_sem.at[pair * gx_count + off],
                device_id=(target, plane),
                device_id_type=pl.DeviceIdType.MESH,
            )
            copy.start()
            copies.append(copy)
        landing[pl.ds(2 * pair, 2), me] = source[pl.ds(2 * pair, 2), me]
        return copies

    def project(pair, values):
        values = apply_matrix(values)
        for side in range(2):
            send_one[2 * pair + side] = values[
                :, side * slab_width : (side + 1) * slab_width
            ].reshape(gx_count, own_rows, slab_width)
        return exchange(pair, send_one, recv_one, one_send, one_recv)

    loads[0].wait()
    load_matrix(dual_ref)
    loads[1].wait()
    first = [project(0, jnp.concatenate([field_ref[0], field_ref[1]], axis=1))]

    gathered[0] = drop_ref[...]
    total_ref[...] = jnp.zeros_like(total_ref)
    for copy in drop_copies:
        copy.wait()
    drops = drop_ref.shape[1]
    block = min(2048, drops)
    blocks = drops // block

    def deposit(step, carry):
        packet = gathered[step // blocks, :, pl.ds(pl.multiple_of(step % blocks * block, 128), block)]
        cell = packet[0:1].astype(jnp.int32)
        mine = packet[1:2].astype(jnp.int32) == plane
        row = jnp.where(mine, cell // slab_width, -1)
        col = cell % slab_width
        hit = lax.broadcasted_iota(jnp.int32, (row_count, block), 0) == row
        left = jnp.where(hit, 1.0, 0.0).astype(jnp.bfloat16)
        here = lax.broadcasted_iota(jnp.int32, (slab_width, block), 0) == col
        terms = []
        for component in range(2):
            rate = packet[2 + component : 3 + component]
            high = rate.astype(jnp.bfloat16).astype(jnp.float32)
            for part in (high, rate - high):
                terms.append(jnp.where(here, part, 0.0).astype(jnp.bfloat16))
        total_ref[...] += product(left, jnp.concatenate(terms, axis=0), transposed=True)
        return carry

    lax.fori_loop(0, gz_count * blocks, deposit, 0)
    merged = []
    for component in range(2):
        base = 2 * component * slab_width
        merged.append(
            field_ref[2 + component]
            + total_ref[:, base : base + slab_width]
            + total_ref[:, base + slab_width : base + 2 * slab_width]
        )
    first.append(project(1, jnp.concatenate(merged, axis=1)))
    loads[2].wait()
    load_matrix(basis_ref)
    across = lax.broadcasted_iota(jnp.int32, (own_rows, row_count), 1)
    down = lax.broadcasted_iota(jnp.int32, (own_rows, row_count), 0) + me * own_rows
    eigen = jnp.sum(jnp.where(across == down, eigen_ref[...], 0.0), axis=1, keepdims=True)
    shift = shift_ref[0]
    weight = aux_ref[4:5, :]
    cos_row = weight * jnp.cos(aux_ref[2:3, :] * shift)
    sin_row = weight * jnp.sin(aux_ref[2:3, :] * shift)
    turned_row = weight * jnp.cos(aux_ref[3:4, :] * shift)
    for copy in loads[3:]:
        copy.wait()
    second = []
    for pair in range(pairs):
        damps = []
        for which in range(2):
            growth = jnp.concatenate(
                [
                    diffusivity_ref[2 * pair + side]
                    * (eigen + aux_ref[which : which + 1, :])
                    for side in range(2)
                ],
                axis=0,
            )
            damps.append((1.0 - growth) / (1.0 + growth))
        cosine = damps[0] * cos_row
        sine = damps[0] * sin_row
        turned = damps[1] * turned_row
        for copy in first[pair]:
            copy.wait()
        rows = jnp.concatenate(
            [
                recv_one[2 * pair : 2 * pair + 2, slab].reshape(2 * own_rows, slab_width)
                for slab in range(gx_count)
            ],
            axis=1,
        )
        high, low = split_two(rows)
        spec = product(high, high_ref[...]) + product(low, high_ref[...])
        spec += product(high, low_ref[...])
        real, imag = spec[:, :half], spec[:, half:]
        spec = jnp.concatenate([real * cosine + imag * sine, imag * turned - real * sine], axis=1)
        high, low = split_two(spec)
        back = product(high, high_ref[...], True) + product(low, high_ref[...], True)
        back += product(high, low_ref[...], True)
        for slab in range(gx_count):
            send_two[2 * pair : 2 * pair + 2, slab] = back[
                :, slab * slab_width : (slab + 1) * slab_width
            ].reshape(2, own_rows, slab_width)
        second.append(exchange(pair, send_two, recv_two, two_send, two_recv))
    for pair in range(pairs):
        for copy in second[pair]:
            copy.wait()
        values = apply_matrix(
            jnp.concatenate(
                [recv_two[2 * pair + side].reshape(row_count, slab_width) for side in range(2)],
                axis=1,
            )
        )
        for side in range(2):
            out_ref[2 * pair + side] = values[:, side * slab_width : (side + 1) * slab_width]


def dense_step(
    field, drop_cell, drop_plane, drop_rate, diffusivity, wall_eigen, basis_part, dual_part, bulk_shift
):
    field_count, _, row_count, slab_width = field.shape
    gx_count = lax.axis_size("gx")
    gz_count = lax.axis_size("gz")
    total = slab_width * gx_count
    half = total // 2
    own_rows = row_count // gx_count
    mode = np.arange(half)
    wave = (2.0 * np.pi / total * mode).astype(np.float32)
    square = wave * wave
    ends = np.where(mode == 0, np.float32(np.pi) ** 2, square).astype(np.float32)
    weight = (np.where(mode == 0, 1.0, 2.0) / total).astype(np.float32)
    late = np.where(mode == 0, np.float32(np.pi), wave).astype(np.float32)
    blank = np.zeros_like(wave)
    aux = np.stack([square, ends, wave, late, weight, blank, blank, blank])
    table = real_table(total)
    high = table.astype(jnp.bfloat16)
    low = (table - high.astype(np.float32)).astype(jnp.bfloat16)
    piece = (field_count, gx_count, own_rows, slab_width)
    vmem = pl.BlockSpec(memory_space=pltpu.VMEM)
    hbm = pl.BlockSpec(memory_space=pl.ANY)
    smem = pl.BlockSpec(memory_space=pltpu.SMEM)
    links = field_count // 2 * gx_count
    drops = drop_cell.shape[0]
    out = pl.pallas_call(
        functools.partial(step_kernel, gx_count, gz_count),
        out_shape=jax.ShapeDtypeStruct((field_count, row_count, slab_width), jnp.float32),
        in_specs=[vmem] * 5 + [smem] * 2 + [hbm] * 5,
        out_specs=vmem,
        scratch_shapes=[
            pltpu.VMEM((field_count, row_count, slab_width), jnp.float32),
            pltpu.VMEM((row_count, row_count), jnp.float32),
            pltpu.VMEM((row_count, row_count), jnp.float32),
            pltpu.VMEM((4, drops), jnp.float32),
            pltpu.VMEM((total, total), jnp.bfloat16),
            pltpu.VMEM((total, total), jnp.bfloat16),
            pltpu.VMEM((row_count, 3 * row_count), jnp.bfloat16),
            pltpu.VMEM((gz_count, 4, drops), jnp.float32),
            pltpu.VMEM((row_count, 4 * slab_width), jnp.float32),
            pltpu.VMEM(piece, jnp.float32),
            pltpu.VMEM(piece, jnp.float32),
            pltpu.VMEM(piece, jnp.float32),
            pltpu.VMEM(piece, jnp.float32),
            pltpu.SemaphoreType.DMA((gz_count,)),
            pltpu.SemaphoreType.DMA((gz_count,)),
            pltpu.SemaphoreType.DMA((links,)),
            pltpu.SemaphoreType.DMA((links,)),
            pltpu.SemaphoreType.DMA((links,)),
            pltpu.SemaphoreType.DMA((links,)),
            pltpu.SemaphoreType.DMA((5,)),
        ],
        compiler_params=pltpu.CompilerParams(
            collective_id=0, has_side_effects=True, vmem_limit_bytes=62 * 2**20
        ),
    )(
        drop_cell[None],
        drop_plane[None],
        drop_rate,
        wall_eigen[None],
        jnp.asarray(aux),
        diffusivity,
        bulk_shift,
        field.reshape(field_count, row_count, slab_width),
        dual_part,
        basis_part,
        jnp.asarray(high),
        jnp.asarray(low),
    )
    return out[:, None]


def deposit_kernel(slab_width, row_ref, col_ref, rate_ref, out_ref):
    rows = out_ref.shape[0]
    depth = row_ref.shape[1]

    @pl.when(pl.program_id(0) == 0)
    def _():
        out_ref[...] = jnp.zeros_like(out_ref)

    hit = lax.broadcasted_iota(jnp.int32, (rows, depth), 0) == row_ref[...]
    left = jnp.where(hit, 1.0, 0.0).astype(jnp.bfloat16)
    here = lax.broadcasted_iota(jnp.int32, (slab_width, depth), 0) == col_ref[...]
    terms = []
    for component in range(2):
        rate = rate_ref[component : component + 1, :]
        high = rate.astype(jnp.bfloat16).astype(jnp.float32)
        for part in (high, rate - high):
            terms.append(jnp.where(here, part, 0.0).astype(jnp.bfloat16))
    right = jnp.concatenate(terms, axis=0)
    out_ref[...] += lax.dot_general(
        left, right, (((1,), (1,)), ((), ())), preferred_element_type=jnp.float32
    )


def deposit(row, col, rate, row_count, slab_width):
    drops = row.shape[1]
    block = min(2048, drops)
    out = pl.pallas_call(
        functools.partial(deposit_kernel, slab_width),
        grid=(drops // block,),
        in_specs=[
            pl.BlockSpec((1, block), lambda i: (0, i)),
            pl.BlockSpec((1, block), lambda i: (0, i)),
            pl.BlockSpec((2, block), lambda i: (0, i)),
        ],
        out_specs=pl.BlockSpec((row_count, 4 * slab_width), lambda i: (0, 0)),
        out_shape=jax.ShapeDtypeStruct((row_count, 4 * slab_width), jnp.float32),
        compiler_params=pltpu.CompilerParams(vmem_limit_bytes=40 * 2**20),
    )(row, col, rate)
    parts = out.reshape(row_count, 2, 2, slab_width).sum(axis=2)
    return parts.transpose(1, 0, 2)


def damping_of(diffusivity, eigen_rows, mode_index, total_cells):
    wavenumber = 2.0 * math.pi / total_cells * mode_index.astype(jnp.float32)
    growth = diffusivity[:, None, None] * (
        eigen_rows[None, :, None] + wavenumber[None, None, :] ** 2
    )
    return (1.0 - growth) / (1.0 + growth)


def per_device(
    field, drop_cell, drop_plane, drop_rate, diffusivity, wall_eigen, basis_part, dual_part, bulk_shift
):
    field_count, _, row_count, slab_width = field.shape
    gx_count = lax.axis_size("gx")
    total = slab_width * gx_count
    own_rows = row_count // gx_count
    half = total // 2
    field = field[:, 0]
    drops = jnp.concatenate(
        [
            drop_cell.astype(jnp.float32)[None],
            drop_plane.astype(jnp.float32)[None],
            drop_rate,
        ]
    )
    drops = lax.all_gather(drops, "gz", axis=1, tiled=True)
    cell = drops[0].astype(jnp.int32)
    mine = drops[1].astype(jnp.int32) == lax.axis_index("gz")
    row = jnp.where(mine, cell // slab_width, -1)[None]
    col = (cell % slab_width)[None]
    source = deposit(row, col, drops[2:], row_count, slab_width)

    def project(matrix, values):
        return values + jnp.einsum("ay,fyx->fax", matrix, values, precision=lax.Precision.HIGH)

    def scatter_rows(values):
        pieces = values.reshape(values.shape[0], gx_count, own_rows, slab_width)
        return lax.all_to_all(pieces, "gx", 1, 1, tiled=True)

    position = lax.axis_index("gx")
    eigen = lax.dynamic_slice(wall_eigen, (position * own_rows,), (own_rows,))
    mode = jnp.arange(half, dtype=jnp.int32)
    damping = damping_of(diffusivity, eigen, mode, total)
    last = damping_of(diffusivity, eigen, jnp.full((1,), half, jnp.int32), total)
    travel = 2.0 * math.pi / total * mode.astype(jnp.float32) * bulk_shift[0]

    def filter_rows(values, first):
        count = values.shape[0]
        damp = damping[first : first + count]
        end = last[first : first + count]
        flat = values.transpose(0, 2, 1, 3).reshape(count, own_rows, total)
        spec = jnp.fft.rfft(flat, axis=-1)
        full = jnp.concatenate([damp, end], axis=-1)
        angle = jnp.append(travel, -math.pi * bulk_shift[0])
        spec = spec * lax.complex(full * jnp.cos(angle), -full * jnp.sin(angle))
        back = jnp.fft.irfft(spec, n=total, axis=-1)
        return back.reshape(count, own_rows, gx_count, slab_width).transpose(0, 2, 1, 3)

    parts = []
    for first, group in ((0, field[:2]), (2, field[2:] + source)):
        rows = scatter_rows(project(dual_part, group))
        back = scatter_rows(filter_rows(rows, first))
        filtered = back.reshape(group.shape)
        parts.append(project(basis_part, filtered))
    return jnp.concatenate(parts)[:, None]


def solution(mesh):
    in_specs = (
        P(None, "gz", None, "gx"),
        P(("gx", "gz")),
        P(("gx", "gz")),
        P(None, ("gx", "gz")),
        P(),
        P(),
        P(),
        P(),
        P(),
    )
    out_specs = P(None, "gz", None, "gx")
    body = dense_step if mesh.shape["gx"] <= DENSE_PARTS else per_device
    return jax.shard_map(
        body, mesh=mesh, in_specs=in_specs, out_specs=out_specs, check_vma=False
    )
```

```python
import functools
import math

import jax
import jax.numpy as jnp
import numpy as np
from jax import lax
from jax.experimental import pallas as pl
from jax.experimental.pallas import tpu as pltpu
from jax.sharding import PartitionSpec as P

DENSE_PARTS = 16


def real_table(total):
    half = total // 2
    product = np.arange(total)[:, None] * np.arange(half)[None, :] % total
    angle = 2.0 * np.pi / total * product
    sines = -np.sin(angle)
    sines[:, 0] = 1.0 - 2.0 * (np.arange(total) % 2)
    return np.concatenate([np.cos(angle), sines], axis=1).astype(np.float32)


def split_two(values):
    high = values.astype(jnp.bfloat16)
    return high, (values - high.astype(jnp.float32)).astype(jnp.bfloat16)


def product(left, right, transposed=False):
    return lax.dot_general(
        left,
        right,
        (((1,), (1 if transposed else 0,)), ((), ())),
        preferred_element_type=jnp.float32,
    )


def step_kernel(
    gx_count,
    gz_count,
    cell_ref,
    plane_ref,
    rate_ref,
    eigen_ref,
    aux_ref,
    diffusivity_ref,
    shift_ref,
    field_hbm,
    dual_hbm,
    basis_hbm,
    high_hbm,
    low_hbm,
    out_ref,
    field_ref,
    dual_ref,
    basis_ref,
    drop_ref,
    high_ref,
    low_ref,
    matrix_ref,
    gathered,
    total_ref,
    send_one,
    recv_one,
    send_two,
    recv_two,
    drop_send,
    drop_recv,
    one_send,
    one_recv,
    two_send,
    two_recv,
    load_sem,
):
    field_count, row_count, slab_width = field_ref.shape
    own_rows = row_count // gx_count
    pairs = field_count // 2
    half = gx_count * slab_width // 2
    me = lax.axis_index("gx")
    plane = lax.axis_index("gz")

    loads = [
        pltpu.make_async_copy(dual_hbm, dual_ref, load_sem.at[0]),
        pltpu.make_async_copy(field_hbm, field_ref, load_sem.at[1]),
        pltpu.make_async_copy(basis_hbm, basis_ref, load_sem.at[2]),
        pltpu.make_async_copy(high_hbm, high_ref, load_sem.at[3]),
        pltpu.make_async_copy(low_hbm, low_ref, load_sem.at[4]),
    ]
    for copy in loads:
        copy.start()
    barrier = pltpu.get_barrier_semaphore()
    for off in range(1, gx_count):
        pl.semaphore_signal(
            barrier,
            inc=1,
            device_id=(lax.rem(me + off, gx_count), plane),
            device_id_type=pl.DeviceIdType.MESH,
        )
    for off in range(1, gz_count):
        pl.semaphore_signal(
            barrier,
            inc=1,
            device_id=(me, lax.rem(plane + off, gz_count)),
            device_id_type=pl.DeviceIdType.MESH,
        )
    drop_ref[0:1] = cell_ref[...].astype(jnp.float32)
    drop_ref[1:2] = plane_ref[...].astype(jnp.float32)
    drop_ref[2:4] = rate_ref[...]
    pl.semaphore_wait(barrier, gx_count + gz_count - 2)

    drop_copies = []
    for off in range(1, gz_count):
        copy = pltpu.make_async_remote_copy(
            src_ref=drop_ref,
            dst_ref=gathered.at[off],
            send_sem=drop_send.at[off],
            recv_sem=drop_recv.at[off],
            device_id=(me, lax.rem(plane + off, gz_count)),
            device_id_type=pl.DeviceIdType.MESH,
        )
        copy.start()
        drop_copies.append(copy)

    def load_matrix(ref):
        high, low = split_two(ref[...])
        matrix_ref[:, :row_count] = high
        matrix_ref[:, row_count : 2 * row_count] = low
        matrix_ref[:, 2 * row_count :] = high

    def apply_matrix(values):
        high, low = split_two(values)
        return values + product(matrix_ref[...], jnp.concatenate([high, high, low], axis=0))

    def exchange(pair, source, landing, send_sem, recv_sem):
        copies = []
        for off in sorted(range(1, gx_count), key=lambda step: abs(2 * step - gx_count)):
            target = lax.rem(me + off, gx_count)
            copy = pltpu.make_async_remote_copy(
                src_ref=source.at[pl.ds(2 * pair, 2), target],
                dst_ref=landing.at[pl.ds(2 * pair, 2), me],
                send_sem=send_sem.at[pair * gx_count + off],
                recv_sem=recv_sem.at[pair * gx_count + off],
                device_id=(target, plane),
                device_id_type=pl.DeviceIdType.MESH,
            )
            copy.start()
            copies.append(copy)
        landing[pl.ds(2 * pair, 2), me] = source[pl.ds(2 * pair, 2), me]
        return copies

    def project(pair, values):
        values = apply_matrix(values)
        for side in range(2):
            send_one[2 * pair + side] = values[
                :, side * slab_width : (side + 1) * slab_width
            ].reshape(gx_count, own_rows, slab_width)
        return exchange(pair, send_one, recv_one, one_send, one_recv)

    loads[0].wait()
    load_matrix(dual_ref)
    loads[1].wait()
    first = [project(0, jnp.concatenate([field_ref[0], field_ref[1]], axis=1))]

    gathered[0] = drop_ref[...]
    total_ref[...] = jnp.zeros_like(total_ref)
    for copy in drop_copies:
        copy.wait_recv()
    drops = drop_ref.shape[1]
    block = min(2048, drops)
    blocks = drops // block

    def deposit(step, carry):
        packet = gathered[step // blocks, :, pl.ds(pl.multiple_of(step % blocks * block, 128), block)]
        cell = packet[0:1].astype(jnp.int32)
        mine = packet[1:2].astype(jnp.int32) == plane
        row = jnp.where(mine, cell // slab_width, -1)
        col = cell % slab_width
        hit = lax.broadcasted_iota(jnp.int32, (row_count, block), 0) == row
        left = jnp.where(hit, 1.0, 0.0).astype(jnp.bfloat16)
        here = lax.broadcasted_iota(jnp.int32, (slab_width, block), 0) == col
        terms = []
        for component in range(2):
            rate = packet[2 + component : 3 + component]
            high = rate.astype(jnp.bfloat16).astype(jnp.float32)
            for part in (high, rate - high):
                terms.append(jnp.where(here, part, 0.0).astype(jnp.bfloat16))
        total_ref[...] += product(left, jnp.concatenate(terms, axis=0), transposed=True)
        return carry

    lax.fori_loop(0, gz_count * blocks, deposit, 0)
    merged = []
    for component in range(2):
        base = 2 * component * slab_width
        merged.append(
            field_ref[2 + component]
            + total_ref[:, base : base + slab_width]
            + total_ref[:, base + slab_width : base + 2 * slab_width]
        )
    first.append(project(1, jnp.concatenate(merged, axis=1)))
    loads[2].wait()
    load_matrix(basis_ref)
    across = lax.broadcasted_iota(jnp.int32, (own_rows, row_count), 1)
    down = lax.broadcasted_iota(jnp.int32, (own_rows, row_count), 0) + me * own_rows
    eigen = jnp.sum(jnp.where(across == down, eigen_ref[...], 0.0), axis=1, keepdims=True)
    shift = shift_ref[0]
    weight = aux_ref[4:5, :]
    cos_row = weight * jnp.cos(aux_ref[2:3, :] * shift)
    sin_row = weight * jnp.sin(aux_ref[2:3, :] * shift)
    turned_row = weight * jnp.cos(aux_ref[3:4, :] * shift)
    for copy in loads[3:]:
        copy.wait()
    second = []
    for pair in range(pairs):
        damps = []
        for which in range(2):
            growth = jnp.concatenate(
                [
                    diffusivity_ref[2 * pair + side]
                    * (eigen + aux_ref[which : which + 1, :])
                    for side in range(2)
                ],
                axis=0,
            )
            damps.append((1.0 - growth) / (1.0 + growth))
        cosine = damps[0] * cos_row
        sine = damps[0] * sin_row
        turned = damps[1] * turned_row
        for copy in first[pair]:
            copy.wait_recv()
        rows = jnp.concatenate(
            [
                recv_one[2 * pair : 2 * pair + 2, slab].reshape(2 * own_rows, slab_width)
                for slab in range(gx_count)
            ],
            axis=1,
        )
        high, low = split_two(rows)
        spec = product(high, high_ref[...]) + product(low, high_ref[...])
        spec += product(high, low_ref[...])
        real, imag = spec[:, :half], spec[:, half:]
        spec = jnp.concatenate([real * cosine + imag * sine, imag * turned - real * sine], axis=1)
        high, low = split_two(spec)
        back = product(high, high_ref[...], True) + product(low, high_ref[...], True)
        back += product(high, low_ref[...], True)
        for slab in range(gx_count):
            send_two[2 * pair : 2 * pair + 2, slab] = back[
                :, slab * slab_width : (slab + 1) * slab_width
            ].reshape(2, own_rows, slab_width)
        second.append(exchange(pair, send_two, recv_two, two_send, two_recv))
    for pair in range(pairs):
        for copy in second[pair]:
            copy.wait_recv()
        values = apply_matrix(
            jnp.concatenate(
                [recv_two[2 * pair + side].reshape(row_count, slab_width) for side in range(2)],
                axis=1,
            )
        )
        for side in range(2):
            out_ref[2 * pair + side] = values[:, side * slab_width : (side + 1) * slab_width]
    for copy in drop_copies + first[0] + first[1] + second[0] + second[1]:
        copy.wait_send()


def dense_step(
    field, drop_cell, drop_plane, drop_rate, diffusivity, wall_eigen, basis_part, dual_part, bulk_shift
):
    field_count, _, row_count, slab_width = field.shape
    gx_count = lax.axis_size("gx")
    gz_count = lax.axis_size("gz")
    total = slab_width * gx_count
    half = total // 2
    own_rows = row_count // gx_count
    mode = np.arange(half)
    wave = (2.0 * np.pi / total * mode).astype(np.float32)
    square = wave * wave
    ends = np.where(mode == 0, np.float32(np.pi) ** 2, square).astype(np.float32)
    weight = (np.where(mode == 0, 1.0, 2.0) / total).astype(np.float32)
    late = np.where(mode == 0, np.float32(np.pi), wave).astype(np.float32)
    blank = np.zeros_like(wave)
    aux = np.stack([square, ends, wave, late, weight, blank, blank, blank])
    table = real_table(total)
    high = table.astype(jnp.bfloat16)
    low = (table - high.astype(np.float32)).astype(jnp.bfloat16)
    piece = (field_count, gx_count, own_rows, slab_width)
    vmem = pl.BlockSpec(memory_space=pltpu.VMEM)
    hbm = pl.BlockSpec(memory_space=pl.ANY)
    smem = pl.BlockSpec(memory_space=pltpu.SMEM)
    links = field_count // 2 * gx_count
    drops = drop_cell.shape[0]
    out = pl.pallas_call(
        functools.partial(step_kernel, gx_count, gz_count),
        out_shape=jax.ShapeDtypeStruct((field_count, row_count, slab_width), jnp.float32),
        in_specs=[vmem] * 5 + [smem] * 2 + [hbm] * 5,
        out_specs=vmem,
        scratch_shapes=[
            pltpu.VMEM((field_count, row_count, slab_width), jnp.float32),
            pltpu.VMEM((row_count, row_count), jnp.float32),
            pltpu.VMEM((row_count, row_count), jnp.float32),
            pltpu.VMEM((4, drops), jnp.float32),
            pltpu.VMEM((total, total), jnp.bfloat16),
            pltpu.VMEM((total, total), jnp.bfloat16),
            pltpu.VMEM((row_count, 3 * row_count), jnp.bfloat16),
            pltpu.VMEM((gz_count, 4, drops), jnp.float32),
            pltpu.VMEM((row_count, 4 * slab_width), jnp.float32),
            pltpu.VMEM(piece, jnp.float32),
            pltpu.VMEM(piece, jnp.float32),
            pltpu.VMEM(piece, jnp.float32),
            pltpu.VMEM(piece, jnp.float32),
            pltpu.SemaphoreType.DMA((gz_count,)),
            pltpu.SemaphoreType.DMA((gz_count,)),
            pltpu.SemaphoreType.DMA((links,)),
            pltpu.SemaphoreType.DMA((links,)),
            pltpu.SemaphoreType.DMA((links,)),
            pltpu.SemaphoreType.DMA((links,)),
            pltpu.SemaphoreType.DMA((5,)),
        ],
        compiler_params=pltpu.CompilerParams(
            collective_id=0, has_side_effects=True, vmem_limit_bytes=62 * 2**20
        ),
    )(
        drop_cell[None],
        drop_plane[None],
        drop_rate,
        wall_eigen[None],
        jnp.asarray(aux),
        diffusivity,
        bulk_shift,
        field.reshape(field_count, row_count, slab_width),
        dual_part,
        basis_part,
        jnp.asarray(high),
        jnp.asarray(low),
    )
    return out[:, None]


def deposit_kernel(slab_width, row_ref, col_ref, rate_ref, out_ref):
    rows = out_ref.shape[0]
    depth = row_ref.shape[1]

    @pl.when(pl.program_id(0) == 0)
    def _():
        out_ref[...] = jnp.zeros_like(out_ref)

    hit = lax.broadcasted_iota(jnp.int32, (rows, depth), 0) == row_ref[...]
    left = jnp.where(hit, 1.0, 0.0).astype(jnp.bfloat16)
    here = lax.broadcasted_iota(jnp.int32, (slab_width, depth), 0) == col_ref[...]
    terms = []
    for component in range(2):
        rate = rate_ref[component : component + 1, :]
        high = rate.astype(jnp.bfloat16).astype(jnp.float32)
        for part in (high, rate - high):
            terms.append(jnp.where(here, part, 0.0).astype(jnp.bfloat16))
    right = jnp.concatenate(terms, axis=0)
    out_ref[...] += lax.dot_general(
        left, right, (((1,), (1,)), ((), ())), preferred_element_type=jnp.float32
    )


def deposit(row, col, rate, row_count, slab_width):
    drops = row.shape[1]
    block = min(2048, drops)
    out = pl.pallas_call(
        functools.partial(deposit_kernel, slab_width),
        grid=(drops // block,),
        in_specs=[
            pl.BlockSpec((1, block), lambda i: (0, i)),
            pl.BlockSpec((1, block), lambda i: (0, i)),
            pl.BlockSpec((2, block), lambda i: (0, i)),
        ],
        out_specs=pl.BlockSpec((row_count, 4 * slab_width), lambda i: (0, 0)),
        out_shape=jax.ShapeDtypeStruct((row_count, 4 * slab_width), jnp.float32),
        compiler_params=pltpu.CompilerParams(vmem_limit_bytes=40 * 2**20),
    )(row, col, rate)
    parts = out.reshape(row_count, 2, 2, slab_width).sum(axis=2)
    return parts.transpose(1, 0, 2)


def damping_of(diffusivity, eigen_rows, mode_index, total_cells):
    wavenumber = 2.0 * math.pi / total_cells * mode_index.astype(jnp.float32)
    growth = diffusivity[:, None, None] * (
        eigen_rows[None, :, None] + wavenumber[None, None, :] ** 2
    )
    return (1.0 - growth) / (1.0 + growth)


def per_device(
    field, drop_cell, drop_plane, drop_rate, diffusivity, wall_eigen, basis_part, dual_part, bulk_shift
):
    field_count, _, row_count, slab_width = field.shape
    gx_count = lax.axis_size("gx")
    total = slab_width * gx_count
    own_rows = row_count // gx_count
    half = total // 2
    field = field[:, 0]
    drops = jnp.concatenate(
        [
            drop_cell.astype(jnp.float32)[None],
            drop_plane.astype(jnp.float32)[None],
            drop_rate,
        ]
    )
    drops = lax.all_gather(drops, "gz", axis=1, tiled=True)
    cell = drops[0].astype(jnp.int32)
    mine = drops[1].astype(jnp.int32) == lax.axis_index("gz")
    row = jnp.where(mine, cell // slab_width, -1)[None]
    col = (cell % slab_width)[None]
    source = deposit(row, col, drops[2:], row_count, slab_width)

    def project(matrix, values):
        return values + jnp.einsum("ay,fyx->fax", matrix, values, precision=lax.Precision.HIGH)

    def scatter_rows(values):
        pieces = values.reshape(values.shape[0], gx_count, own_rows, slab_width)
        return lax.all_to_all(pieces, "gx", 1, 1, tiled=True)

    position = lax.axis_index("gx")
    eigen = lax.dynamic_slice(wall_eigen, (position * own_rows,), (own_rows,))
    mode = jnp.arange(half, dtype=jnp.int32)
    damping = damping_of(diffusivity, eigen, mode, total)
    last = damping_of(diffusivity, eigen, jnp.full((1,), half, jnp.int32), total)
    travel = 2.0 * math.pi / total * mode.astype(jnp.float32) * bulk_shift[0]

    def filter_rows(values, first):
        count = values.shape[0]
        damp = damping[first : first + count]
        end = last[first : first + count]
        flat = values.transpose(0, 2, 1, 3).reshape(count, own_rows, total)
        spec = jnp.fft.rfft(flat, axis=-1)
        full = jnp.concatenate([damp, end], axis=-1)
        angle = jnp.append(travel, -math.pi * bulk_shift[0])
        spec = spec * lax.complex(full * jnp.cos(angle), -full * jnp.sin(angle))
        back = jnp.fft.irfft(spec, n=total, axis=-1)
        return back.reshape(count, own_rows, gx_count, slab_width).transpose(0, 2, 1, 3)

    parts = []
    for first, group in ((0, field[:2]), (2, field[2:] + source)):
        rows = scatter_rows(project(dual_part, group))
        back = scatter_rows(filter_rows(rows, first))
        filtered = back.reshape(group.shape)
        parts.append(project(basis_part, filtered))
    return jnp.concatenate(parts)[:, None]


def solution(mesh):
    in_specs = (
        P(None, "gz", None, "gx"),
        P(("gx", "gz")),
        P(("gx", "gz")),
        P(None, ("gx", "gz")),
        P(),
        P(),
        P(),
        P(),
        P(),
    )
    out_specs = P(None, "gz", None, "gx")
    body = dense_step if mesh.shape["gx"] <= DENSE_PARTS else per_device
    return jax.shard_map(
        body, mesh=mesh, in_specs=in_specs, out_specs=out_specs, check_vma=False
    )
```

```python
import functools
import math

import jax
import jax.numpy as jnp
import numpy as np
from jax import lax
from jax.experimental import pallas as pl
from jax.experimental.pallas import tpu as pltpu
from jax.sharding import PartitionSpec as P

DENSE_PARTS = 16


def real_table(total):
    half = total // 2
    product = np.arange(total)[:, None] * np.arange(half)[None, :] % total
    angle = 2.0 * np.pi / total * product
    sines = -np.sin(angle)
    sines[:, 0] = 1.0 - 2.0 * (np.arange(total) % 2)
    return np.concatenate([np.cos(angle), sines], axis=1).astype(np.float32)


def split_two(values):
    high = values.astype(jnp.bfloat16)
    return high, (values - high.astype(jnp.float32)).astype(jnp.bfloat16)


def product(left, right, transposed=False):
    return lax.dot_general(
        left,
        right,
        (((1,), (1 if transposed else 0,)), ((), ())),
        preferred_element_type=jnp.float32,
    )


def step_kernel(
    gx_count,
    gz_count,
    cell_ref,
    plane_ref,
    rate_ref,
    eigen_ref,
    aux_ref,
    diffusivity_ref,
    shift_ref,
    field_hbm,
    dual_hbm,
    basis_hbm,
    high_hbm,
    low_hbm,
    out_ref,
    field_ref,
    dual_ref,
    basis_ref,
    drop_ref,
    high_ref,
    low_ref,
    matrix_ref,
    gathered,
    total_ref,
    send_one,
    recv_one,
    send_two,
    recv_two,
    drop_send,
    drop_recv,
    one_send,
    one_recv,
    two_send,
    two_recv,
    load_sem,
):
    field_count, row_count, slab_width = field_ref.shape
    own_rows = row_count // gx_count
    pairs = field_count // 2
    half = gx_count * slab_width // 2
    me = lax.axis_index("gx")
    plane = lax.axis_index("gz")

    loads = [
        pltpu.make_async_copy(dual_hbm, dual_ref, load_sem.at[0]),
        pltpu.make_async_copy(field_hbm, field_ref, load_sem.at[1]),
        pltpu.make_async_copy(basis_hbm, basis_ref, load_sem.at[2]),
        pltpu.make_async_copy(high_hbm, high_ref, load_sem.at[3]),
        pltpu.make_async_copy(low_hbm, low_ref, load_sem.at[4]),
    ]
    for copy in loads:
        copy.start()
    barrier = pltpu.get_barrier_semaphore()
    for off in range(1, gx_count):
        pl.semaphore_signal(
            barrier,
            inc=1,
            device_id=(lax.rem(me + off, gx_count), plane),
            device_id_type=pl.DeviceIdType.MESH,
        )
    for off in range(1, gz_count):
        pl.semaphore_signal(
            barrier,
            inc=1,
            device_id=(me, lax.rem(plane + off, gz_count)),
            device_id_type=pl.DeviceIdType.MESH,
        )
    drop_ref[0:1] = cell_ref[...].astype(jnp.float32)
    drop_ref[1:2] = plane_ref[...].astype(jnp.float32)
    drop_ref[2:4] = rate_ref[...]
    pl.semaphore_wait(barrier, gx_count + gz_count - 2)

    drop_copies = []
    for off in range(1, gz_count):
        copy = pltpu.make_async_remote_copy(
            src_ref=drop_ref,
            dst_ref=gathered.at[off],
            send_sem=drop_send.at[off],
            recv_sem=drop_recv.at[off],
            device_id=(me, lax.rem(plane + off, gz_count)),
            device_id_type=pl.DeviceIdType.MESH,
        )
        copy.start()
        drop_copies.append(copy)

    def load_matrix(ref):
        high, low = split_two(ref[...])
        matrix_ref[:, :row_count] = high
        matrix_ref[:, row_count : 2 * row_count] = low
        matrix_ref[:, 2 * row_count :] = high

    def apply_matrix(values):
        high, low = split_two(values)
        return values + product(matrix_ref[...], jnp.concatenate([high, high, low], axis=0))

    def exchange(pair, source, landing, send_sem, recv_sem):
        copies = []
        for off in range(1, gx_count):
            target = lax.rem(me + off, gx_count)
            copy = pltpu.make_async_remote_copy(
                src_ref=source.at[pl.ds(2 * pair, 2), target],
                dst_ref=landing.at[pl.ds(2 * pair, 2), me],
                send_sem=send_sem.at[pair * gx_count + off],
                recv_sem=recv_sem.at[pair * gx_count + off],
                device_id=(target, plane),
                device_id_type=pl.DeviceIdType.MESH,
            )
            copy.start()
            copies.append(copy)
        landing[pl.ds(2 * pair, 2), me] = source[pl.ds(2 * pair, 2), me]
        return copies

    def project(pair, values):
        values = apply_matrix(values)
        for side in range(2):
            send_one[2 * pair + side] = values[
                :, side * slab_width : (side + 1) * slab_width
            ].reshape(gx_count, own_rows, slab_width)
        return exchange(pair, send_one, recv_one, one_send, one_recv)

    loads[0].wait()
    load_matrix(dual_ref)
    loads[1].wait()
    first = [project(0, jnp.concatenate([field_ref[0], field_ref[1]], axis=1))]

    gathered[0] = drop_ref[...]
    total_ref[...] = jnp.zeros_like(total_ref)
    for copy in drop_copies:
        copy.wait()
    drops = drop_ref.shape[1]
    block = min(4096, drops)
    blocks = drops // block

    def deposit(step, carry):
        packet = gathered[step // blocks, :, pl.ds(pl.multiple_of(step % blocks * block, 128), block)]
        cell = packet[0:1].astype(jnp.int32)
        mine = packet[1:2].astype(jnp.int32) == plane
        row = jnp.where(mine, cell // slab_width, -1)
        col = cell % slab_width
        hit = lax.broadcasted_iota(jnp.int32, (row_count, block), 0) == row
        left = jnp.where(hit, 1.0, 0.0).astype(jnp.bfloat16)
        here = lax.broadcasted_iota(jnp.int32, (slab_width, block), 0) == col
        terms = []
        for component in range(2):
            rate = packet[2 + component : 3 + component]
            high = rate.astype(jnp.bfloat16).astype(jnp.float32)
            for part in (high, rate - high):
                terms.append(jnp.where(here, part, 0.0).astype(jnp.bfloat16))
        total_ref[...] += product(left, jnp.concatenate(terms, axis=0), transposed=True)
        return carry

    lax.fori_loop(0, gz_count * blocks, deposit, 0)
    merged = []
    for component in range(2):
        base = 2 * component * slab_width
        merged.append(
            field_ref[2 + component]
            + total_ref[:, base : base + slab_width]
            + total_ref[:, base + slab_width : base + 2 * slab_width]
        )
    first.append(project(1, jnp.concatenate(merged, axis=1)))
    loads[2].wait()
    load_matrix(basis_ref)
    across = lax.broadcasted_iota(jnp.int32, (own_rows, row_count), 1)
    down = lax.broadcasted_iota(jnp.int32, (own_rows, row_count), 0) + me * own_rows
    eigen = jnp.sum(jnp.where(across == down, eigen_ref[...], 0.0), axis=1, keepdims=True)
    shift = shift_ref[0]
    weight = aux_ref[4:5, :]
    cos_row = weight * jnp.cos(aux_ref[2:3, :] * shift)
    sin_row = weight * jnp.sin(aux_ref[2:3, :] * shift)
    turned_row = weight * jnp.cos(aux_ref[3:4, :] * shift)
    for copy in loads[3:]:
        copy.wait()
    second = []
    for pair in range(pairs):
        damps = []
        for which in range(2):
            growth = jnp.concatenate(
                [
                    diffusivity_ref[2 * pair + side]
                    * (eigen + aux_ref[which : which + 1, :])
                    for side in range(2)
                ],
                axis=0,
            )
            damps.append((1.0 - growth) / (1.0 + growth))
        cosine = damps[0] * cos_row
        sine = damps[0] * sin_row
        turned = damps[1] * turned_row
        for copy in first[pair]:
            copy.wait()
        rows = jnp.concatenate(
            [
                recv_one[2 * pair : 2 * pair + 2, slab].reshape(2 * own_rows, slab_width)
                for slab in range(gx_count)
            ],
            axis=1,
        )
        high, low = split_two(rows)
        spec = product(high, high_ref[...]) + product(low, high_ref[...])
        spec += product(high, low_ref[...])
        real, imag = spec[:, :half], spec[:, half:]
        spec = jnp.concatenate([real * cosine + imag * sine, imag * turned - real * sine], axis=1)
        high, low = split_two(spec)
        back = product(high, high_ref[...], True) + product(low, high_ref[...], True)
        back += product(high, low_ref[...], True)
        for slab in range(gx_count):
            send_two[2 * pair : 2 * pair + 2, slab] = back[
                :, slab * slab_width : (slab + 1) * slab_width
            ].reshape(2, own_rows, slab_width)
        second.append(exchange(pair, send_two, recv_two, two_send, two_recv))
    for pair in range(pairs):
        for copy in second[pair]:
            copy.wait()
        values = apply_matrix(
            jnp.concatenate(
                [recv_two[2 * pair + side].reshape(row_count, slab_width) for side in range(2)],
                axis=1,
            )
        )
        for side in range(2):
            out_ref[2 * pair + side] = values[:, side * slab_width : (side + 1) * slab_width]


def dense_step(
    field, drop_cell, drop_plane, drop_rate, diffusivity, wall_eigen, basis_part, dual_part, bulk_shift
):
    field_count, _, row_count, slab_width = field.shape
    gx_count = lax.axis_size("gx")
    gz_count = lax.axis_size("gz")
    total = slab_width * gx_count
    half = total // 2
    own_rows = row_count // gx_count
    mode = np.arange(half)
    wave = (2.0 * np.pi / total * mode).astype(np.float32)
    square = wave * wave
    ends = np.where(mode == 0, np.float32(np.pi) ** 2, square).astype(np.float32)
    weight = (np.where(mode == 0, 1.0, 2.0) / total).astype(np.float32)
    late = np.where(mode == 0, np.float32(np.pi), wave).astype(np.float32)
    blank = np.zeros_like(wave)
    aux = np.stack([square, ends, wave, late, weight, blank, blank, blank])
    table = real_table(total)
    high = table.astype(jnp.bfloat16)
    low = (table - high.astype(np.float32)).astype(jnp.bfloat16)
    piece = (field_count, gx_count, own_rows, slab_width)
    vmem = pl.BlockSpec(memory_space=pltpu.VMEM)
    hbm = pl.BlockSpec(memory_space=pl.ANY)
    smem = pl.BlockSpec(memory_space=pltpu.SMEM)
    links = field_count // 2 * gx_count
    drops = drop_cell.shape[0]
    out = pl.pallas_call(
        functools.partial(step_kernel, gx_count, gz_count),
        out_shape=jax.ShapeDtypeStruct((field_count, row_count, slab_width), jnp.float32),
        in_specs=[vmem] * 5 + [smem] * 2 + [hbm] * 5,
        out_specs=vmem,
        scratch_shapes=[
            pltpu.VMEM((field_count, row_count, slab_width), jnp.float32),
            pltpu.VMEM((row_count, row_count), jnp.float32),
            pltpu.VMEM((row_count, row_count), jnp.float32),
            pltpu.VMEM((4, drops), jnp.float32),
            pltpu.VMEM((total, total), jnp.bfloat16),
            pltpu.VMEM((total, total), jnp.bfloat16),
            pltpu.VMEM((row_count, 3 * row_count), jnp.bfloat16),
            pltpu.VMEM((gz_count, 4, drops), jnp.float32),
            pltpu.VMEM((row_count, 4 * slab_width), jnp.float32),
            pltpu.VMEM(piece, jnp.float32),
            pltpu.VMEM(piece, jnp.float32),
            pltpu.VMEM(piece, jnp.float32),
            pltpu.VMEM(piece, jnp.float32),
            pltpu.SemaphoreType.DMA((gz_count,)),
            pltpu.SemaphoreType.DMA((gz_count,)),
            pltpu.SemaphoreType.DMA((links,)),
            pltpu.SemaphoreType.DMA((links,)),
            pltpu.SemaphoreType.DMA((links,)),
            pltpu.SemaphoreType.DMA((links,)),
            pltpu.SemaphoreType.DMA((5,)),
        ],
        compiler_params=pltpu.CompilerParams(
            collective_id=0, has_side_effects=True, vmem_limit_bytes=62 * 2**20
        ),
    )(
        drop_cell[None],
        drop_plane[None],
        drop_rate,
        wall_eigen[None],
        jnp.asarray(aux),
        diffusivity,
        bulk_shift,
        field.reshape(field_count, row_count, slab_width),
        dual_part,
        basis_part,
        jnp.asarray(high),
        jnp.asarray(low),
    )
    return out[:, None]


def deposit_kernel(slab_width, row_ref, col_ref, rate_ref, out_ref):
    rows = out_ref.shape[0]
    depth = row_ref.shape[1]

    @pl.when(pl.program_id(0) == 0)
    def _():
        out_ref[...] = jnp.zeros_like(out_ref)

    hit = lax.broadcasted_iota(jnp.int32, (rows, depth), 0) == row_ref[...]
    left = jnp.where(hit, 1.0, 0.0).astype(jnp.bfloat16)
    here = lax.broadcasted_iota(jnp.int32, (slab_width, depth), 0) == col_ref[...]
    terms = []
    for component in range(2):
        rate = rate_ref[component : component + 1, :]
        high = rate.astype(jnp.bfloat16).astype(jnp.float32)
        for part in (high, rate - high):
            terms.append(jnp.where(here, part, 0.0).astype(jnp.bfloat16))
    right = jnp.concatenate(terms, axis=0)
    out_ref[...] += lax.dot_general(
        left, right, (((1,), (1,)), ((), ())), preferred_element_type=jnp.float32
    )


def deposit(row, col, rate, row_count, slab_width):
    drops = row.shape[1]
    block = min(2048, drops)
    out = pl.pallas_call(
        functools.partial(deposit_kernel, slab_width),
        grid=(drops // block,),
        in_specs=[
            pl.BlockSpec((1, block), lambda i: (0, i)),
            pl.BlockSpec((1, block), lambda i: (0, i)),
            pl.BlockSpec((2, block), lambda i: (0, i)),
        ],
        out_specs=pl.BlockSpec((row_count, 4 * slab_width), lambda i: (0, 0)),
        out_shape=jax.ShapeDtypeStruct((row_count, 4 * slab_width), jnp.float32),
        compiler_params=pltpu.CompilerParams(vmem_limit_bytes=40 * 2**20),
    )(row, col, rate)
    parts = out.reshape(row_count, 2, 2, slab_width).sum(axis=2)
    return parts.transpose(1, 0, 2)


def damping_of(diffusivity, eigen_rows, mode_index, total_cells):
    wavenumber = 2.0 * math.pi / total_cells * mode_index.astype(jnp.float32)
    growth = diffusivity[:, None, None] * (
        eigen_rows[None, :, None] + wavenumber[None, None, :] ** 2
    )
    return (1.0 - growth) / (1.0 + growth)


def per_device(
    field, drop_cell, drop_plane, drop_rate, diffusivity, wall_eigen, basis_part, dual_part, bulk_shift
):
    field_count, _, row_count, slab_width = field.shape
    gx_count = lax.axis_size("gx")
    total = slab_width * gx_count
    own_rows = row_count // gx_count
    half = total // 2
    field = field[:, 0]
    drops = jnp.concatenate(
        [
            drop_cell.astype(jnp.float32)[None],
            drop_plane.astype(jnp.float32)[None],
            drop_rate,
        ]
    )
    drops = lax.all_gather(drops, "gz", axis=1, tiled=True)
    cell = drops[0].astype(jnp.int32)
    mine = drops[1].astype(jnp.int32) == lax.axis_index("gz")
    row = jnp.where(mine, cell // slab_width, -1)[None]
    col = (cell % slab_width)[None]
    source = deposit(row, col, drops[2:], row_count, slab_width)

    def project(matrix, values):
        return values + jnp.einsum("ay,fyx->fax", matrix, values, precision=lax.Precision.HIGH)

    def scatter_rows(values):
        pieces = values.reshape(values.shape[0], gx_count, own_rows, slab_width)
        return lax.all_to_all(pieces, "gx", 1, 1, tiled=True)

    position = lax.axis_index("gx")
    eigen = lax.dynamic_slice(wall_eigen, (position * own_rows,), (own_rows,))
    mode = jnp.arange(half, dtype=jnp.int32)
    damping = damping_of(diffusivity, eigen, mode, total)
    last = damping_of(diffusivity, eigen, jnp.full((1,), half, jnp.int32), total)
    travel = 2.0 * math.pi / total * mode.astype(jnp.float32) * bulk_shift[0]

    def filter_rows(values, first):
        count = values.shape[0]
        damp = damping[first : first + count]
        end = last[first : first + count]
        flat = values.transpose(0, 2, 1, 3).reshape(count, own_rows, total)
        spec = jnp.fft.rfft(flat, axis=-1)
        full = jnp.concatenate([damp, end], axis=-1)
        angle = jnp.append(travel, -math.pi * bulk_shift[0])
        spec = spec * lax.complex(full * jnp.cos(angle), -full * jnp.sin(angle))
        back = jnp.fft.irfft(spec, n=total, axis=-1)
        return back.reshape(count, own_rows, gx_count, slab_width).transpose(0, 2, 1, 3)

    parts = []
    for first, group in ((0, field[:2]), (2, field[2:] + source)):
        rows = scatter_rows(project(dual_part, group))
        back = scatter_rows(filter_rows(rows, first))
        filtered = back.reshape(group.shape)
        parts.append(project(basis_part, filtered))
    return jnp.concatenate(parts)[:, None]


def solution(mesh):
    in_specs = (
        P(None, "gz", None, "gx"),
        P(("gx", "gz")),
        P(("gx", "gz")),
        P(None, ("gx", "gz")),
        P(),
        P(),
        P(),
        P(),
        P(),
    )
    out_specs = P(None, "gz", None, "gx")
    body = dense_step if mesh.shape["gx"] <= DENSE_PARTS else per_device
    return jax.shard_map(
        body, mesh=mesh, in_specs=in_specs, out_specs=out_specs, check_vma=False
    )
```
